32 devices in a mesh: expert: 4 (over y, x), tensor: 8 (over z, core).
Axes of the slice: x: 2, y: 2, z: 4, core: 2. Of those that a mesh axis runs over, the one named last changes fastest.
Arguments:
- expert_hidden: bfloat16 [4, 768, 8192], P('expert', 'tensor'), may hold values from -6 to 6
- probe_tangent: bfloat16 [4, 6144, 8192], P('expert', 'tensor'), may hold values from -0.0625 to 0.0625
- routed_experts: int32 [768, 2], P('expert'), may hold values from 0 to 3, all different within a row; in each aligned block of 192 rows (0 to 191, 192 to 383, ...) at most 192 rows name the same one
- gate_weights: float32 [768, 2], P('expert'), may hold values from 0.1 to 1
Outputs:
- ggn_product: bfloat16 [4, 6144, 8192], P('expert', 'tensor')
- token_quadratic: float32 [768], P('expert')
The draws below stay inside these ranges and needn't reach their ends.
Inputs may be any that keep to these rules, and one draw needn't show every extreme that they name: `routed_experts`: each row names two different experts. Among the 192 rows of one source, no expert is named by more than 192 rows, a bound that some block reaches.
All inputs are finite; a program needn't handle non-finite values.
Results may differ from the reference program's by a relative error of at most 0.0057.
Values may be sent and summed in bfloat16 or wider, within the bound.
A program may use at most 128 MiB of HBM per device.

```python
import math
import jax
import jax.numpy as jnp
import numpy as np
from jax import lax

D = 6144
FF = 8192
TOK_DEV = 192
EXPERTS = 4
CAP = 192
ROWS = 768
TOKENS = 768
N_EXPERT = 4


def block_scale(own_key, extent, split, smallest, top_value):
    def one(dim, parts):
        draws = jax.random.uniform(jax.random.fold_in(jax.random.fold_in(own_key, 6), dim), (parts,), jnp.float32, smallest / len(split), top_value / len(split))
        return jnp.repeat(jnp.exp(draws), extent[dim] // parts).reshape((-1,) + (1,) * (len(extent) - dim - 1))

    loudness = one(*split[0])
    for cut in split[1:]:
        loudness = loudness * one(*cut)
    return loudness


def deal_out(key, own, number, rows, number_of, top, most, lean):
    ranking = jax.random.permutation(key, number_of)
    crowded, ordinary = load_shares(number_of, rows * top, most, lean, True), load_shares(number_of, rows * top, most, lean, False)
    places = jnp.arange(number_of)

    def named(lengths, turn):
        used = int((lengths > 0).sum())
        fixed = max(1, used // 4)
        moved = fixed + (places - fixed + turn * (used - fixed)) % max(1, number_of - fixed)
        return jnp.zeros((number_of,), jnp.int32).at[ranking[jnp.where(places < fixed, places, moved)]].set(jnp.asarray(lengths, jnp.int32))

    lengths = jnp.where(number % 4 == 0, named(crowded, number // 4), named(ordinary, number - number // 4 - 1))
    mixed = jax.random.permutation(jax.random.fold_in(own, 3), number_of)
    donor, receiver = mixed[0:number_of // 2 * 2:2], mixed[1:number_of // 2 * 2:2]
    margin = jnp.minimum(lengths[donor] - 1, most - lengths[receiver]) // 2
    margin = jnp.where((donor == ranking[0]) | (receiver == ranking[0]) | (lengths[receiver] == 0), 0, jnp.maximum(margin, 0))
    moved = jax.random.randint(jax.random.fold_in(own, 4), (number_of // 2,), 0, 1 << 20) % (margin + 1)
    lengths = lengths.at[donor].add(-moved).at[receiver].add(moved)
    members = jnp.searchsorted(jnp.cumsum(lengths), jnp.arange(rows * top), side="right").astype(jnp.int32)
    table = members.reshape(top, rows).T
    table = table[jax.random.permutation(jax.random.fold_in(own, 1), rows)]
    turn = jax.random.randint(jax.random.fold_in(own, 2), (rows, 1), 0, top)
    return jnp.take_along_axis(table, (jnp.arange(top)[None, :] + turn) % top, axis=1)


def load_shares(count, total, most, lean, full):
    weights = [(1 << 20) // math.isqrt(rank ** lean) + 1 for rank in range(1, count + 1)]
    largest = most if full else min(most, max(-(-total // count), total * weights[0] // sum(weights)))
    least = 1 if total - largest >= count - 1 else 0
    counts, rest = [largest] + [least] * (count - 1), total - largest - least * (count - 1)
    while rest > 0:
        candidates = [i for i in range(1, count) if counts[i] < largest] or [i for i in range(1, count) if counts[i] < most]
        pool, remaining = sum([weights[i] for i in candidates]), rest
        for i in candidates:
            extra = min(most - counts[i], max(1, remaining * weights[i] // pool), rest)
            counts[i] = counts[i] + extra
            rest = rest - extra
    return np.array(counts)


def scatter_about(rng, dims, width, bound, pieces=(), kind=jnp.bfloat16):
    entries = jax.random.normal(rng, dims, jnp.float32) * width
    if len(pieces) > 0:
        entries = block_scale(rng, dims, pieces, -0.22, 0.18) * entries
    return jnp.clip(entries, min=-bound, max=bound).astype(kind)


def setup_inputs(seed: int = 0) -> dict:
    streams_of = jax.random.split(jax.random.key(seed), 5)
    expert_hidden = scatter_about(streams_of[0], (EXPERTS, ROWS, FF), 1.0, 6.0, ((0, 4), (1, 8)))
    probe_tangent = scatter_about(streams_of[1], (EXPERTS, D, FF), FF ** -0.5, 0.0625, ((0, 4), (1, 8)))
    routed_experts_keys = jax.random.split(jax.random.fold_in(streams_of[2], 1), TOKENS // TOK_DEV)
    routed_experts_turns = jax.random.permutation(jax.random.fold_in(streams_of[2], 3), TOKENS // TOK_DEV)
    routed_experts = jax.vmap(lambda own, number: deal_out(jax.random.fold_in(streams_of[2], 2), own, number, TOK_DEV, EXPERTS, 2, CAP, 2))(routed_experts_keys, routed_experts_turns).reshape((TOKENS, 2))
    gate_weights = jnp.clip(0.1 + 0.9 * jax.random.uniform(streams_of[3], (TOKENS, 2), jnp.float32) ** block_scale(streams_of[3], (TOKENS, 2), ((0, 4),), -0.2, 0.2), 0.1, 1.0)
    return dict(expert_hidden=expert_hidden, probe_tangent=probe_tangent, routed_experts=routed_experts, gate_weights=gate_weights)


def expert_forward(operands):
    hidden_rows, probe_rows = operands
    return jnp.dot(hidden_rows, probe_rows.T, preferred_element_type=jnp.float32).astype(jnp.bfloat16)


def expert_backward(operands):
    returned_rows, hidden_rows = operands
    return jnp.dot(returned_rows.T, hidden_rows, preferred_element_type=jnp.float32).astype(jnp.bfloat16)


def reference(expert_hidden, probe_tangent, routed_experts, gate_weights):
    pair_count = TOK_DEV * 2
    source_ids = routed_experts.reshape(N_EXPERT, pair_count).astype(jnp.int32)
    expert_range = jnp.arange(N_EXPERT, dtype=jnp.int32)
    one_hot = (source_ids[:, :, None] == expert_range[None, None, :]).astype(jnp.int32)
    earlier = (jnp.cumsum(one_hot, axis=1).astype(jnp.int32) - one_hot).astype(jnp.int32)
    slot_rank = jnp.sum(one_hot * earlier, axis=2).astype(jnp.int32)
    buffer_row = (jnp.arange(N_EXPERT, dtype=jnp.int32)[:, None] * CAP + slot_rank).astype(jnp.int32)
    expert_flat = source_ids.reshape(-1)
    row_flat = buffer_row.reshape(-1)
    gate_flat = gate_weights.reshape(-1)

    expert_tangent = lax.map(expert_forward, (expert_hidden, probe_tangent))
    picked = expert_tangent[expert_flat, row_flat].astype(jnp.float32) * gate_flat[:, None]
    token_tangent = jnp.sum(picked.reshape(TOKENS, 2, D), axis=1)
    token_quadratic = jnp.sum(token_tangent * token_tangent, axis=1) / D

    weighted = (token_tangent[:, None, :] * gate_weights[:, :, None]).reshape(TOKENS * 2, D).astype(jnp.bfloat16)
    returned = jnp.zeros((N_EXPERT, ROWS, D), jnp.bfloat16).at[expert_flat, row_flat].set(weighted)
    ggn_product = lax.map(expert_backward, (returned, expert_hidden))
    return ggn_product, token_quadratic
```

```python
import jax
import jax.numpy as jnp
from jax import lax
from jax.sharding import PartitionSpec as P


def local(expert_hidden, probe_tangent, routed_experts, gate_weights):
    expert_count = lax.axis_size("expert")
    tensor_count = lax.axis_size("tensor")
    hidden_local = expert_hidden[0]
    probe_local = probe_tangent[0]
    col_count = probe_local.shape[0]
    tok_count = routed_experts.shape[0]
    capacity = hidden_local.shape[0] * tensor_count // expert_count
    ids_flat = routed_experts.reshape(-1)
    gate_flat = gate_weights.reshape(-1)
    one_hot = (ids_flat[:, None] == jnp.arange(expert_count, dtype=jnp.int32)[None, :]).astype(
        jnp.int32
    )
    pair = jnp.arange(ids_flat.shape[0], dtype=jnp.int32)
    earlier = jnp.dot(
        (pair[None, :] < pair[:, None]).astype(jnp.bfloat16),
        one_hot.astype(jnp.bfloat16),
        preferred_element_type=jnp.float32,
    ).astype(jnp.int32)
    slot_rank = jnp.sum(one_hot * earlier, axis=1)
    buffer_row = ids_flat * capacity + slot_rank
    hidden_all = lax.all_gather(hidden_local, "tensor", axis=0, tiled=True)
    expert_tangent = lax.dot_general(
        hidden_all, probe_local, (((1,), (1,)), ((), ())), preferred_element_type=jnp.float32
    ).astype(jnp.bfloat16)
    outgoing = expert_tangent.reshape(expert_count, capacity, col_count)
    received = lax.all_to_all(outgoing, "expert", split_axis=0, concat_axis=0, tiled=True)
    block_cols = received.shape[2]
    flat_rows = received.reshape(expert_count * capacity, block_cols)
    picked = flat_rows[buffer_row].astype(jnp.float32) * gate_flat[:, None]
    token_tangent = jnp.sum(picked.reshape(tok_count, 2, block_cols), axis=1)
    weighted = (token_tangent[:, None, :] * gate_weights[:, :, None]).reshape(
        tok_count * 2, block_cols
    )
    weighted = weighted.astype(jnp.bfloat16)
    buffer = (
        jnp.zeros((expert_count * capacity, block_cols), jnp.bfloat16).at[buffer_row].set(weighted)
    )
    buffer, token_tangent = (buffer, token_tangent)
    returning = lax.all_to_all(
        buffer.reshape(expert_count, capacity, col_count),
        "expert",
        split_axis=0,
        concat_axis=0,
        tiled=True,
    )
    returning_flat = returning.reshape(expert_count * capacity, col_count)
    gradient = lax.dot_general(
        returning_flat, hidden_all, (((0,), (0,)), ((), ())), preferred_element_type=jnp.float32
    ).astype(jnp.bfloat16)
    partial_squares = jnp.sum(token_tangent * token_tangent, axis=1)
    total_squares = lax.psum(partial_squares, "tensor")
    token_quadratic = total_squares / (col_count * tensor_count)
    return (gradient[None], token_quadratic)


def solution(mesh):
    placed = (
        P("expert", "tensor", None),
        P("expert", "tensor", None),
        P("expert", None),
        P("expert", None),
    )
    return jax.shard_map(
        local,
        mesh=mesh,
        in_specs=placed,
        out_specs=(P("expert", "tensor", None), P("expert")),
        check_vma=False,
    )
```
